128 devices in a mesh: row: 8 (over x_hi, y), col: 16 (over x_lo, z, core).
Axes of the slice: x: 4 (x_hi: 2, x_lo: 2; x = x_hi * 2 + x_lo), y: 4, z: 4, core: 2. Of those that a mesh axis runs over, the one named last changes fastest.
Arguments:
- tokens: bfloat16 [8192, 12288], P('row', 'col'), may hold values from -6 to 6
- joined_weight: bfloat16 [12288, 8192], P('row', 'col'), may hold values from -0.0546875 to 0.0546875
- positions: int32 [8192], P('row'), may hold values from 0 to 8191
Outputs:
- queries: bfloat16 [8192, 6144], P(('row', 'col'))
- rotated_keys: bfloat16 [8192, 1024], P(('row', 'col'))
- values: bfloat16 [8192, 1024], P(('row', 'col'))
The draws below stay inside these ranges and needn't reach their ends.
All inputs are finite; a program needn't handle non-finite values.
Results may differ from the reference program's by a relative error of at most 0.001.
Values may be sent and summed in bfloat16 or wider, within the bound.
No kernel may reach another device: no remote copies, remote signals or barrier semaphores. Data moves between devices by JAX's collectives and lax.ppermute only.
A program may use at most 128 MiB of HBM per device.

```python
import math
import jax
import jax.numpy as jnp

D = 12288
HEAD_WIDTH = 128
QUERY_HEADS = 48
KEY_VALUE_HEADS = 8
TOKENS = 8192
JOINED = 8192


def place_ends(result, key, smallest, top_value):
    longest = result.shape.index(max(result.shape))
    spots = []
    for shift in (0, 1):
        where = [jax.random.randint(jax.random.fold_in(key, axis), (), 0, length) for axis, length in enumerate(result.shape)]
        where[longest] = (where[longest] + shift) % result.shape[longest]
        spots.append(tuple(where))
    return result.at[spots[0]].set(smallest).at[spots[1]].set(top_value)


def shard_levels(own_key, dims, split, smallest, largest):
    gain, own = 1.0, jax.random.fold_in(own_key, 6)
    for dim, parts in split:
        heights = jnp.exp(jax.random.uniform(jax.random.fold_in(own, dim), (parts,), jnp.float32, smallest / len(split), largest / len(split)))
        gain = gain * jnp.repeat(heights, dims[dim] // parts).reshape([-1 if axis == dim else 1 for axis in range(len(dims))])
    return gain


def centred(own_key, shape, deviation, limit, cuts=(), kind=jnp.bfloat16):
    drawn = deviation * jax.random.normal(own_key, shape, jnp.float32)
    if cuts:
        drawn = drawn * shard_levels(own_key, shape, cuts, -0.22, 0.18)
    return jnp.clip(drawn, -limit, limit).astype(kind)


def setup_inputs(seed: int = 0) -> dict:
    key_of = jax.random.split(jax.random.key(seed), 4)
    tokens = centred(key_of[0], (TOKENS, D), 1.0, 6.0, ((0, 8), (1, 16)))
    joined_weight = centred(key_of[1], (D, JOINED), D ** -0.5, 0.0546875, ((0, 8), (1, 16)))
    positions = place_ends(jax.random.randint(key_of[2], (TOKENS,), 0, 8192), jax.random.fold_in(key_of[2], 1), 0, 8191).astype(jnp.int32)
    return dict(tokens=tokens, joined_weight=joined_weight, positions=positions)


rope_base = 1000000.0


def rotary_tables(positions, head_size):
    half_size = head_size // 2
    column_ids = jnp.arange(head_size, dtype=jnp.int32)
    exponent = (column_ids % half_size).astype(jnp.float32) * (-2.0 * math.log(rope_base) / head_size)
    frequency = jnp.exp(exponent)
    angles = positions.astype(jnp.float32)[:, None] * frequency[None, :]
    sign_table = jnp.where(column_ids < half_size, -1.0, 1.0).astype(jnp.float32)
    return jnp.cos(angles), jnp.sin(angles) * sign_table[None, :]


def rotate(head_groups, positions):
    cosine, sine_table = rotary_tables(positions, head_groups.shape[-1])
    swapped = jnp.roll(head_groups, head_groups.shape[-1] // 2, axis=-1)
    return head_groups * cosine[:, None, :] + swapped * sine_table[:, None, :]


def reference(tokens, joined_weight, positions):
    projected_rows = jnp.dot(tokens, joined_weight, preferred_element_type=jnp.float32)
    token_total = projected_rows.shape[0]
    rotated_columns = (QUERY_HEADS + KEY_VALUE_HEADS) * HEAD_WIDTH
    head_groups = projected_rows[:, :rotated_columns].reshape(token_total, QUERY_HEADS + KEY_VALUE_HEADS, HEAD_WIDTH)
    turned = rotate(head_groups, positions).reshape(token_total, rotated_columns)
    queries = turned[:, :QUERY_HEADS * HEAD_WIDTH].astype(jnp.bfloat16)
    rotated_keys = turned[:, QUERY_HEADS * HEAD_WIDTH:].astype(jnp.bfloat16)
    values = projected_rows[:, rotated_columns:].astype(jnp.bfloat16)
    return (queries, rotated_keys, values)
```

```python
import math

import jax
import jax.numpy as jnp
import numpy as np
from jax import lax
from jax.experimental import pallas as pl
from jax.experimental.pallas import tpu as pltpu
from jax.sharding import Mesh
from jax.sharding import PartitionSpec as P

HEAD_WIDTH = 128
QUERY_HEADS = 48
KEY_VALUE_HEADS = 8

rope_base = 1000000.0
SWAP = ((0, 1), (1, 0))


def rotary_tables(positions, head_size):
    half_size = head_size // 2
    column_ids = jnp.arange(head_size, dtype=jnp.int32)
    exponent = (column_ids % half_size).astype(jnp.float32) * (
        -2.0 * math.log(rope_base) / head_size
    )
    frequency = jnp.exp(exponent)
    angles = positions.astype(jnp.float32)[:, None] * frequency[None, :]
    sign_table = jnp.where(column_ids < half_size, -1.0, 1.0).astype(jnp.float32)
    return (jnp.cos(angles), jnp.sin(angles) * sign_table[None, :])


def ring_step(block, axis):
    pairs = [
        (i * 2 + c, ((i + (1, -1)[c]) % 4) * 2 + c) for i in range(4) for c in range(2)
    ]
    return lax.ppermute(block, (axis, "c"), pairs)


def ring(block, axis):
    blocks = [block]
    for _ in range(3):
        blocks.append(ring_step(blocks[-1], axis))
    return blocks


def piece_table():
    table = np.zeros((2, 4, 2, 4, 2, 16, 2), np.int32)
    for xh in range(2):
        for y in range(4):
            for xl in range(2):
                for z in range(4):
                    for c in range(2):
                        rows = []
                        for which in range(2):
                            half = c if which == 0 else 1 - c
                            toward = 1 if half == 0 else -1
                            for partner in range(2):
                                for step in range(4):
                                    block = (xl ^ partner, (z - toward * step) % 4)
                                    own = 1 if c == 0 else -1
                                    b_step = ((y - block[1]) * own) % 4
                                    b_partner = xh ^ block[0]
                                    late = max(partner * 4 + step, b_partner * 4 + b_step)
                                    rows.append(
                                        (late, which * 8 + partner * 4 + step, (b_partner * 4 + b_step) * 2 + half)
                                    )
                        rows.sort()
                        table[xh, y, xl, z, c] = [r[1:] for r in rows]
    return table


TABLE = piece_table()


def product(table, first, count, a_pieces, b_pieces, total=None, tables=None):
    chunks = len(a_pieces[0])
    chunk_rows, depth = a_pieces[0][0].shape
    rows = chunk_rows * chunks
    columns = b_pieces[0].shape[1]
    n_a, n_b = len(a_pieces), len(b_pieces)
    slots = 3
    tile = 256
    last = tables is not None

    def kernel(table_ref, *refs):
        a_refs = [refs[p * chunks : (p + 1) * chunks] for p in range(n_a)]
        refs = refs[n_a * chunks :]
        b_refs, refs = refs[:n_b], refs[n_b:]
        if total is not None:
            total_ref, refs = refs[0], refs[1:]
        if last:
            (cos_ref, sin_ref), refs = refs[:2], refs[2:]
        out_ref, a_buf, b_buf, acc, sems = refs

        def start(k):
            slot = lax.rem(k, slots)
            a_id = table_ref[(first + k) * 2]
            b_id = table_ref[(first + k) * 2 + 1]
            for p in range(n_a):

                @pl.when(a_id == p)
                def _():
                    for j in range(chunks):
                        pltpu.make_async_copy(
                            a_refs[p][j],
                            a_buf.at[slot, pl.ds(j * chunk_rows, chunk_rows), :],
                            sems.at[slot, j],
                        ).start()

            for q in range(n_b):

                @pl.when(b_id == q)
                def _():
                    pltpu.make_async_copy(b_refs[q], b_buf.at[slot], sems.at[slot, chunks]).start()

        def wait(k):
            slot = lax.rem(k, slots)
            for j in range(chunks):
                part = a_buf.at[slot, pl.ds(j * chunk_rows, chunk_rows), :]
                pltpu.make_async_copy(part, part, sems.at[slot, j]).wait()
            pltpu.make_async_copy(b_buf.at[slot], b_buf.at[slot], sems.at[slot, chunks]).wait()

        def spans(body):
            @pl.loop(0, rows // tile)
            def _(i):
                body(pl.ds(pl.multiple_of(i * tile, tile), tile))

        sum_ref = acc if last else out_ref

        @pl.loop(0, slots - 1)
        def _(k):
            start(k)

        def begin(span):
            if total is None:
                sum_ref[span, :] = jnp.zeros((tile, columns), jnp.float32)
            else:
                sum_ref[span, :] = total_ref[span, :]

        spans(begin)

        @pl.loop(0, count)
        def _(k):
            wait(k)

            @pl.when(k + slots - 1 < count)
            def _():
                start(k + slots - 1)

            slot = lax.rem(k, slots)

            def add(span):
                sum_ref[span, :] += jnp.dot(
                    a_buf[slot, span, :], b_buf[slot], preferred_element_type=jnp.float32
                )

            spans(add)

        def turn(span):
            cosine, sine = cos_ref[span, :], sin_ref[span, :]
            for h in range(columns // HEAD_WIDTH):
                head = acc[span, h * HEAD_WIDTH : (h + 1) * HEAD_WIDTH]
                swapped = pltpu.roll(head, HEAD_WIDTH // 2, 1)
                out_ref[span, h * HEAD_WIDTH : (h + 1) * HEAD_WIDTH] = (
                    head * cosine + swapped * sine
                ).astype(jnp.bfloat16)

        if last:
            spans(turn)

    anywhere = pl.BlockSpec(memory_space=pl.ANY)
    vmem = pl.BlockSpec(memory_space=pltpu.VMEM)
    operands = [table.reshape(-1)]
    in_specs = [pl.BlockSpec(memory_space=pltpu.SMEM)]
    for piece in a_pieces:
        operands += piece
        in_specs += [anywhere] * chunks
    operands += b_pieces
    in_specs += [anywhere] * n_b
    if total is not None:
        operands.append(total)
        in_specs.append(vmem)
    if last:
        operands += tables
        in_specs += [vmem] * 2
    return pl.pallas_call(
        kernel,
        out_shape=jax.ShapeDtypeStruct((rows, columns), jnp.bfloat16 if last else jnp.float32),
        in_specs=in_specs,
        out_specs=vmem,
        scratch_shapes=[
            pltpu.VMEM((slots, rows, depth), a_pieces[0][0].dtype),
            pltpu.VMEM((slots, depth, columns), b_pieces[0].dtype),
            pltpu.VMEM((rows, columns), jnp.float32),
            pltpu.SemaphoreType.DMA((slots, chunks + 1)),
        ],
        compiler_params=pltpu.CompilerParams(vmem_limit_bytes=24 * 1024 * 1024),
        cost_estimate=pl.CostEstimate(
            flops=2 * rows * columns * depth * count,
            bytes_accessed=(rows + columns) * depth * 2 * count,
            transcendentals=0,
        ),
    )(*operands)


CHUNKS = 2


def shards(tokens, joined_weight, positions):
    rows, depth = tokens.shape
    columns = joined_weight.shape[1]
    place = [lax.axis_index(a) for a in ("xh", "y", "xl", "z", "c")]
    table = jnp.asarray(TABLE)[tuple(place)]

    part = rows // CHUNKS
    a_chunks, b_chunks = [], []
    for k in range(CHUNKS):
        own = tokens[k * part : (k + 1) * part]
        a_chunks.append(ring(own, "z") + ring(lax.ppermute(own, "xl", SWAP), "z"))
    for k in range(2):
        own = joined_weight[k * depth : (k + 1) * depth]
        b_chunks.append(ring(own, "y") + ring(lax.ppermute(own, "xh", SWAP), "y"))
    a_pieces = [[a_chunks[k][i] for k in range(CHUNKS)] for i in range(8)]
    a_pieces += [[lax.ppermute(v, "c", SWAP) for v in piece] for piece in a_pieces]
    b_pieces = [b_chunks[k][i] for i in range(8) for k in range(2)]

    column_block = (place[2] * 4 + place[3]) * 2 + place[4]
    rotated = column_block * columns < (QUERY_HEADS + KEY_VALUE_HEADS) * HEAD_WIDTH
    cosine, sine = rotary_tables(positions, HEAD_WIDTH)
    tables = [jnp.where(rotated, cosine, 1.0), jnp.where(rotated, sine, 0.0)]

    turned = product(table, 0, 16, a_pieces, b_pieces, None, tables)
    received = lax.all_to_all(turned, ("xl", "z", "c"), split_axis=0, concat_axis=1, tiled=True)
    query_columns = QUERY_HEADS * HEAD_WIDTH
    rotated_columns = (QUERY_HEADS + KEY_VALUE_HEADS) * HEAD_WIDTH
    return (
        received[:, :query_columns],
        received[:, query_columns:rotated_columns],
        received[:, rotated_columns:],
    )


def solution(mesh):
    fine = Mesh(mesh.devices.reshape(2, 4, 2, 4, 2), ("xh", "y", "xl", "z", "c"))
    row, col = ("xh", "y"), ("xl", "z", "c")
    in_specs = (P(row, col), P(row, col), P(row))
    out_specs = (P(row + col, None),) * 3
    return jax.shard_map(shards, mesh=fine, in_specs=in_specs, out_specs=out_specs, check_vma=False)
```

```python
import math

import jax
import jax.numpy as jnp
import numpy as np
from jax import lax
from jax.experimental import pallas as pl
from jax.experimental.pallas import tpu as pltpu
from jax.sharding import Mesh
from jax.sharding import PartitionSpec as P

HEAD_WIDTH = 128
QUERY_HEADS = 48
KEY_VALUE_HEADS = 8

rope_base = 1000000.0
SWAP = ((0, 1), (1, 0))


def rotary_tables(positions, head_size):
    half_size = head_size // 2
    column_ids = jnp.arange(head_size, dtype=jnp.int32)
    exponent = (column_ids % half_size).astype(jnp.float32) * (
        -2.0 * math.log(rope_base) / head_size
    )
    frequency = jnp.exp(exponent)
    angles = positions.astype(jnp.float32)[:, None] * frequency[None, :]
    sign_table = jnp.where(column_ids < half_size, -1.0, 1.0).astype(jnp.float32)
    return (jnp.cos(angles), jnp.sin(angles) * sign_table[None, :])


def ring_step(block, axis, way=1):
    pairs = [
        (i * 2 + c, ((i + (1, -1)[c] * way) % 4) * 2 + c) for i in range(4) for c in range(2)
    ]
    return lax.ppermute(block, (axis, "c"), pairs)


def piece_table():
    table = np.zeros((2, 4, 2, 4, 2, 8, 2), np.int32)
    for xh, y, xl, z, c in np.ndindex(2, 4, 2, 4, 2):
        way = (1, -1)[c]
        places = (0, -way, way, 2)
        a_blocks = {(xl ^ p, (z + d) % 4): p * 4 + i for p in range(2) for i, d in enumerate(places)}
        b_blocks = {(xh ^ p, (y + d) % 4): p * 4 + i for p in range(2) for i, d in enumerate(places)}
        pairs = [(a_blocks[f], b_blocks[f]) for f in np.ndindex(2, 4)]
        table[xh, y, xl, z, c] = sorted(pairs, key=lambda p: (7 in p, max(p), p))
    return table


TABLE = piece_table()
EARLY = 6


def product(table, core, first, count, a_blocks, b_blocks, total=None, tables=None):
    rows = sum(v.shape[0] for v in a_blocks[0][0])
    half = a_blocks[0][0][0].shape[1]
    depth, columns = 2 * half, b_blocks[0][0].shape[1]
    slots = 2
    tile = 256
    last = tables is not None
    used_a = [p for p in range(len(a_blocks)) if a_blocks[p] is not None]
    used_b = [q for q in range(len(b_blocks)) if b_blocks[q] is not None]

    def kernel(table_ref, *refs):
        refs = list(refs)
        a_refs = {p: [[refs.pop(0) for _ in part] for part in a_blocks[p]] for p in used_a}
        b_refs = {q: [refs.pop(0) for _ in b_blocks[q]] for q in used_b}
        if total is not None:
            total_ref = refs.pop(0)
        if last:
            cos_ref, sin_ref = refs.pop(0), refs.pop(0)
        out_ref, a_buf, b_buf, *rest, sems = refs
        acc = rest[0] if last else out_ref
        me = table_ref[16]

        def start(k):
            slot = lax.rem(k, slots)
            a_id = table_ref[(first + k) * 2]
            b_id = table_ref[(first + k) * 2 + 1]
            for p in used_a:

                @pl.when(a_id == p)
                def _():
                    for part in range(2):
                        own = me if part == 0 else 1 - me
                        span = pl.ds(pl.multiple_of(own * half, half), half)
                        row = 0
                        for ref in a_refs[p][part]:
                            pltpu.make_async_copy(
                                ref, a_buf.at[slot, pl.ds(row, ref.shape[0]), span], sems.at[slot]
                            ).start()
                            row += ref.shape[0]

            for q in used_b:

                @pl.when(b_id == q)
                def _():
                    row = 0
                    for ref in b_refs[q]:
                        pltpu.make_async_copy(
                            ref, b_buf.at[slot, pl.ds(row, ref.shape[0]), :], sems.at[slot]
                        ).start()
                        row += ref.shape[0]

        def wait(k):
            slot = lax.rem(k, slots)
            pltpu.make_async_copy(a_buf.at[slot], a_buf.at[slot], sems.at[slot]).wait()
            pltpu.make_async_copy(b_buf.at[slot], b_buf.at[slot], sems.at[slot]).wait()

        def spans(body):
            @pl.loop(0, rows // tile)
            def _(i):
                body(pl.ds(pl.multiple_of(i * tile, tile), tile))

        start(0)
        if total is None:
            acc[...] = jnp.zeros(acc.shape, jnp.float32)
        elif last:
            acc[...] = total_ref[...]

        @pl.loop(0, count)
        def _(k):
            @pl.when(k + 1 < count)
            def _():
                start(k + 1)

            wait(k)
            slot = lax.rem(k, slots)
            acc[...] += jnp.dot(a_buf[slot], b_buf[slot], preferred_element_type=jnp.float32)

        def turn(span):
            cosine, sine = cos_ref[span, :], sin_ref[span, :]
            for h in range(columns // HEAD_WIDTH):
                head = acc[span, h * HEAD_WIDTH : (h + 1) * HEAD_WIDTH]
                swapped = pltpu.roll(head, HEAD_WIDTH // 2, 1)
                out_ref[span, h * HEAD_WIDTH : (h + 1) * HEAD_WIDTH] = (
                    head * cosine + swapped * sine
                ).astype(jnp.bfloat16)

        if last:
            spans(turn)

    anywhere = pl.BlockSpec(memory_space=pl.ANY)
    vmem = pl.BlockSpec(memory_space=pltpu.VMEM)
    pieces = [v for p in used_a for part in a_blocks[p] for v in part]
    pieces += [v for q in used_b for v in b_blocks[q]]
    operands = [jnp.concatenate([table.reshape(-1), core.reshape(1)])]
    operands += [pltpu.with_memory_space_constraint(v, pltpu.HBM) for v in pieces]
    in_specs = [pl.BlockSpec(memory_space=pltpu.SMEM)] + [anywhere] * len(pieces)
    if total is not None:
        operands.append(total)
        in_specs.append(vmem)
    if last:
        operands += tables
        in_specs += [vmem] * 2
    scratch = [
        pltpu.VMEM((slots, rows, depth), pieces[0].dtype),
        pltpu.VMEM((slots, depth, columns), pieces[0].dtype),
    ]
    if last:
        scratch.append(pltpu.VMEM((rows, columns), jnp.float32))
    return pl.pallas_call(
        kernel,
        out_shape=jax.ShapeDtypeStruct((rows, columns), jnp.bfloat16 if last else jnp.float32),
        in_specs=in_specs,
        out_specs=vmem,
        scratch_shapes=scratch + [pltpu.SemaphoreType.DMA((slots,))],
        compiler_params=pltpu.CompilerParams(vmem_limit_bytes=28 * 1024 * 1024),
        cost_estimate=pl.CostEstimate(
            flops=2 * rows * columns * depth * count,
            bytes_accessed=(rows + columns) * depth * 2 * count,
            transcendentals=0,
        ),
    )(*operands)


def after(block, *before):
    return lax.optimization_barrier((block,) + before)[0]


def swap(block, axis):
    return lax.ppermute(block, axis, SWAP)


def gathers(a, b):
    a_part, b_part = a.shape[0] // 2, b.shape[0] // 2
    a_0, a_1, b_0, b_1 = a[:a_part], a[a_part:], b[:b_part], b[b_part:]

    z_near, z_other = ring_step(a, "z"), ring_step(a, "z", -1)
    y_near, y_other = ring_step(b, "y"), ring_step(b, "y", -1)
    p_0 = swap(a_0, "xl")
    r_0 = swap(after(b_0, p_0), "xh")

    p_0_in = after(p_0, z_near, z_other, r_0)
    r_0_in = after(r_0, y_near, y_other)
    p_0_near, p_0_other = ring_step(p_0_in, "z"), ring_step(p_0_in, "z", -1)
    r_0_near, r_0_other = ring_step(r_0_in, "y"), ring_step(r_0_in, "y", -1)
    p_1 = swap(after(a_1, z_near, z_other, y_near, y_other), "xl")
    r_1 = swap(after(b_1, p_1), "xh")

    z_far = ring_step(after(z_near, p_0_near, p_0_other), "z")
    y_far = ring_step(after(y_near, r_0_near, r_0_other), "y")
    a_c = swap(after(a, p_0_near, p_0_other, r_0_near, r_0_other), "c")
    z_near_c = swap(after(z_near, a_c), "c")
    z_other_c = swap(after(z_other, z_near_c), "c")

    p_1_in = after(p_1, z_far, r_1)
    r_1_in = after(r_1, y_far)
    p_1_near, p_1_other = ring_step(p_1_in, "z"), ring_step(p_1_in, "z", -1)
    r_1_near, r_1_other = ring_step(r_1_in, "y"), ring_step(r_1_in, "y", -1)
    p_0_c = swap(after(p_0, z_far, y_far), "c")
    p_0_near_c = swap(after(p_0_near, p_0_c), "c")
    p_0_other_c = swap(after(p_0_other, p_0_near_c), "c")
    z_far_c = swap(after(z_far, p_0_other_c), "c")

    p_0_far = ring_step(after(p_0_near, p_1_near, p_1_other), "z")
    r_0_far = ring_step(after(r_0_near, r_1_near, r_1_other), "y")
    p_1_far = ring_step(p_1_near, "z")
    r_1_far = ring_step(r_1_near, "y")
    p_1_c = swap(after(p_1, p_1_near, p_1_other, r_1_near, r_1_other), "c")
    p_1_near_c = swap(after(p_1_near, p_1_c), "c")
    p_1_other_c = swap(after(p_1_other, p_1_near_c), "c")
    p_0_far_c = swap(p_0_far, "c")
    p_1_far_c = swap(p_1_far, "c")

    a_blocks = [
        ([a], [a_c]),
        ([z_near], [z_other_c]),
        ([z_other], [z_near_c]),
        ([z_far], [z_far_c]),
        ([p_0, p_1], [p_0_c, p_1_c]),
        ([p_0_near, p_1_near], [p_0_other_c, p_1_other_c]),
        ([p_0_other, p_1_other], [p_0_near_c, p_1_near_c]),
        ([p_0_far, p_1_far], [p_0_far_c, p_1_far_c]),
    ]
    b_blocks = [
        [b],
        [y_near],
        [y_other],
        [y_far],
        [r_0, r_1],
        [r_0_near, r_1_near],
        [r_0_other, r_1_other],
        [r_0_far, r_1_far],
    ]
    return a_blocks, b_blocks


def shards(tokens, joined_weight, positions):
    rows, depth = tokens.shape
    columns = joined_weight.shape[1]
    place = [lax.axis_index(a) for a in ("xh", "y", "xl", "z", "c")]
    table = jnp.asarray(TABLE)[tuple(place)]

    a_blocks, b_blocks = gathers(tokens, joined_weight)

    column_block = (place[2] * 4 + place[3]) * 2 + place[4]
    rotated = column_block * columns < (QUERY_HEADS + KEY_VALUE_HEADS) * HEAD_WIDTH
    cosine, sine = rotary_tables(positions, HEAD_WIDTH)
    tables = [jnp.where(rotated, cosine, 1.0), jnp.where(rotated, sine, 0.0)]

    early = product(table, place[4], 0, EARLY, a_blocks[:7] + [None], b_blocks[:7] + [None])
    turned = product(table, place[4], EARLY, 8 - EARLY, a_blocks, b_blocks, early, tables)
    received = lax.all_to_all(turned, ("xl", "z", "c"), split_axis=0, concat_axis=1, tiled=True)
    query_columns = QUERY_HEADS * HEAD_WIDTH
    rotated_columns = (QUERY_HEADS + KEY_VALUE_HEADS) * HEAD_WIDTH
    return (
        received[:, :query_columns],
        received[:, query_columns:rotated_columns],
        received[:, rotated_columns:],
    )


def solution(mesh):
    fine = Mesh(mesh.devices.reshape(2, 4, 2, 4, 2), ("xh", "y", "xl", "z", "c"))
    row, col = ("xh", "y"), ("xl", "z", "c")
    in_specs = (P(row, col), P(row, col), P(row))
    out_specs = (P(row + col, None),) * 3
    return jax.shard_map(shards, mesh=fine, in_specs=in_specs, out_specs=out_specs, check_vma=False)
```

```python
import math

import jax
import jax.numpy as jnp
import numpy as np
from jax import lax
from jax.experimental import pallas as pl
from jax.experimental.pallas import tpu as pltpu
from jax.sharding import Mesh
from jax.sharding import PartitionSpec as P

HEAD_WIDTH = 128
QUERY_HEADS = 48
KEY_VALUE_HEADS = 8

rope_base = 1000000.0
SWAP = ((0, 1), (1, 0))


def rotary_tables(positions, head_size):
    half_size = head_size // 2
    column_ids = jnp.arange(head_size, dtype=jnp.int32)
    exponent = (column_ids % half_size).astype(jnp.float32) * (
        -2.0 * math.log(rope_base) / head_size
    )
    frequency = jnp.exp(exponent)
    angles = positions.astype(jnp.float32)[:, None] * frequency[None, :]
    sign_table = jnp.where(column_ids < half_size, -1.0, 1.0).astype(jnp.float32)
    return (jnp.cos(angles), jnp.sin(angles) * sign_table[None, :])


def ring_step(block, axis, way=1):
    pairs = [
        (i * 2 + c, ((i + (1, -1)[c] * way) % 4) * 2 + c) for i in range(4) for c in range(2)
    ]
    return lax.ppermute(block, (axis, "c"), pairs)


def piece_table():
    table = np.zeros((2, 4, 2, 4, 2, 8, 2), np.int32)
    for xh, y, xl, z, c in np.ndindex(2, 4, 2, 4, 2):
        way = (1, -1)[c]
        places = (0, -way, way, 2)
        a_blocks = {(xl ^ p, (z + d) % 4): p * 4 + i for p in range(2) for i, d in enumerate(places)}
        b_blocks = {(xh ^ p, (y + d) % 4): p * 4 + i for p in range(2) for i, d in enumerate(places)}
        pairs = [(a_blocks[f], b_blocks[f]) for f in np.ndindex(2, 4)]
        table[xh, y, xl, z, c] = sorted(pairs, key=lambda p: (7 in p, max(p), p))
    return table


TABLE = piece_table()
EARLY = 6


def product(table, first, count, a_blocks, b_blocks, parts, totals=()):
    depth = a_blocks[0][0].shape[1]
    rows = sum(v.shape[0] for v in a_blocks[0])
    width = b_blocks[0].shape[1] // 2
    slots = 2
    used_a = [p for p in range(len(a_blocks)) if a_blocks[p] is not None]
    used_b = [q for q in range(len(b_blocks)) if b_blocks[q] is not None]
    low, high = parts[0] * width, (parts[-1] + 1) * width

    def kernel(table_ref, *refs):
        refs = list(refs)
        a_refs = {p: [refs.pop(0) for _ in a_blocks[p]] for p in used_a}
        b_refs = {q: refs.pop(0) for q in used_b}
        total_refs = [refs.pop(0) for _ in totals]
        out_refs = [refs.pop(0) for _ in parts]
        a_buf, b_buf, sems = refs

        def start(k):
            slot = lax.rem(k, slots)
            a_id = table_ref[(first + k) * 2]
            b_id = table_ref[(first + k) * 2 + 1]
            for p in used_a:

                @pl.when(a_id == p)
                def _():
                    row = 0
                    for ref in a_refs[p]:
                        pltpu.make_async_copy(
                            ref, a_buf.at[slot, pl.ds(row, ref.shape[0]), :], sems.at[slot]
                        ).start()
                        row += ref.shape[0]

            for q in used_b:

                @pl.when(b_id == q)
                def _():
                    pltpu.make_async_copy(
                        b_refs[q].at[:, pl.ds(low, high - low)], b_buf.at[slot], sems.at[slot]
                    ).start()

        def wait(k):
            slot = lax.rem(k, slots)
            pltpu.make_async_copy(a_buf.at[slot], a_buf.at[slot], sems.at[slot]).wait()
            pltpu.make_async_copy(b_buf.at[slot], b_buf.at[slot], sems.at[slot]).wait()

        start(0)
        if totals:
            out_refs[0][...] = sum(ref[...] for ref in total_refs)
        else:
            for ref in out_refs:
                ref[...] = jnp.zeros(ref.shape, jnp.float32)

        @pl.loop(0, count)
        def _(k):
            @pl.when(k + 1 < count)
            def _():
                start(k + 1)

            wait(k)
            slot = lax.rem(k, slots)
            for i, ref in enumerate(out_refs):
                ref[...] += jnp.dot(
                    a_buf[slot],
                    b_buf[slot, :, i * width : (i + 1) * width],
                    preferred_element_type=jnp.float32,
                )

    anywhere = pl.BlockSpec(memory_space=pl.ANY)
    vmem = pl.BlockSpec(memory_space=pltpu.VMEM)
    pieces = [v for p in used_a for v in a_blocks[p]] + [b_blocks[q] for q in used_b]
    late = [7 in used_a and p == 7 for p in used_a for _ in a_blocks[p]] + [q == 7 for q in used_b]
    operands = [table.reshape(-1)]
    operands += [
        pltpu.with_memory_space_constraint(v, pltpu.VMEM if near else pltpu.HBM)
        for v, near in zip(pieces, late)
    ]
    return pl.pallas_call(
        kernel,
        out_shape=[jax.ShapeDtypeStruct((rows, width), jnp.float32) for _ in parts],
        in_specs=[pl.BlockSpec(memory_space=pltpu.SMEM)] + [anywhere] * len(pieces) + [vmem] * len(totals),
        out_specs=[vmem] * len(parts),
        scratch_shapes=[
            pltpu.VMEM((slots, rows, depth), pieces[0].dtype),
            pltpu.VMEM((slots, depth, high - low), pieces[0].dtype),
            pltpu.SemaphoreType.DMA((slots,)),
        ],
        compiler_params=pltpu.CompilerParams(vmem_limit_bytes=24 * 1024 * 1024),
        cost_estimate=pl.CostEstimate(
            flops=2 * rows * (high - low) * depth * count,
            bytes_accessed=(rows + high - low) * depth * 2 * count,
            transcendentals=0,
        ),
    )(*operands, *totals)


def turn(total, received, cosine, sine):
    rows, columns = total.shape
    tile = 256

    def kernel(total_ref, received_ref, cos_ref, sin_ref, out_ref):
        @pl.loop(0, rows // tile)
        def _(i):
            span = pl.ds(pl.multiple_of(i * tile, tile), tile)
            for h in range(columns // HEAD_WIDTH):
                lanes = slice(h * HEAD_WIDTH, (h + 1) * HEAD_WIDTH)
                head = total_ref[span, lanes] + received_ref[span, lanes]
                swapped = pltpu.roll(head, HEAD_WIDTH // 2, 1)
                out_ref[span, lanes] = (head * cos_ref[span, :] + swapped * sin_ref[span, :]).astype(
                    jnp.bfloat16
                )

    return pl.pallas_call(
        kernel,
        out_shape=jax.ShapeDtypeStruct((rows, columns), jnp.bfloat16),
        compiler_params=pltpu.CompilerParams(vmem_limit_bytes=24 * 1024 * 1024),
        cost_estimate=pl.CostEstimate(flops=rows * columns * 4, bytes_accessed=rows * columns * 12, transcendentals=0),
    )(total, received, cosine, sine)


def after(block, *before):
    return lax.optimization_barrier((block,) + before)[0]


def swap(block, axis):
    return lax.ppermute(block, axis, SWAP)


def gathers(a, b):
    part = a.shape[0] // 2

    z_near, z_other = ring_step(a, "z"), ring_step(a, "z", -1)
    y_near, y_other = ring_step(b, "y"), ring_step(b, "y", -1)
    r = swap(b, "xh")

    p_0 = swap(after(a[:part], r), "xl")
    r_in = after(r, y_near, y_other)
    r_near, r_other = ring_step(r_in, "y"), ring_step(r_in, "y", -1)
    z_far = ring_step(after(z_near, z_other, r), "z")

    p_0_in = after(p_0, z_far)
    p_0_near, p_0_other = ring_step(p_0_in, "z"), ring_step(p_0_in, "z", -1)
    p_1 = swap(after(a[part:], p_0, z_far), "xl")

    y_far = ring_step(after(y_near, r_near, r_other, p_1, p_0_near, p_0_other), "y")
    p_1_in = after(p_1, p_0_near, p_0_other)
    p_1_near, p_1_other = ring_step(p_1_in, "z"), ring_step(p_1_in, "z", -1)

    r_far = ring_step(after(r_near, y_far), "y")
    p_0_far = ring_step(after(p_0_near, p_1_near, p_1_other), "z")
    p_1_far = ring_step(after(p_1_near, p_1_other), "z")

    a_blocks = [
        [a],
        [z_near],
        [z_other],
        [z_far],
        [p_0, p_1],
        [p_0_near, p_1_near],
        [p_0_other, p_1_other],
        [p_0_far, p_1_far],
    ]
    return a_blocks, [b, y_near, y_other, y_far, r, r_near, r_other, r_far]


def shards(tokens, joined_weight, positions):
    rows, depth = tokens.shape
    columns = joined_weight.shape[1]
    place = [lax.axis_index(a) for a in ("xh", "y", "xl", "z", "c")]
    table = jnp.asarray(TABLE)[tuple(place)]

    core = place[4]
    mine = lax.dynamic_slice_in_dim(joined_weight, core * depth, depth, 0)
    sent = lax.dynamic_slice_in_dim(joined_weight, (1 - core) * depth, depth, 0)
    weight = jnp.concatenate([mine, swap(sent, "c")], axis=1)
    a_blocks, b_blocks = gathers(tokens, weight)

    column_block = (place[2] * 4 + place[3]) * 2 + place[4]
    rotated = column_block * columns < (QUERY_HEADS + KEY_VALUE_HEADS) * HEAD_WIDTH
    cosine, sine = rotary_tables(positions, HEAD_WIDTH)
    cosine, sine = jnp.where(rotated, cosine, 1.0), jnp.where(rotated, sine, 0.0)

    early_a, early_b = a_blocks[:7] + [None], b_blocks[:7] + [None]
    early, early_sent = product(table, 0, EARLY, early_a, early_b, (0, 1))
    early_received = swap(early_sent, "c")
    (late_sent,) = product(table, EARLY, 8 - EARLY, a_blocks, b_blocks, (1,))
    late_received = swap(late_sent, "c")
    (total,) = product(table, EARLY, 8 - EARLY, a_blocks, b_blocks, (0,), (early, early_received))
    turned = turn(total, late_received, cosine, sine)
    received = lax.all_to_all(turned, ("xl", "z", "c"), split_axis=0, concat_axis=1, tiled=True)
    query_columns = QUERY_HEADS * HEAD_WIDTH
    rotated_columns = (QUERY_HEADS + KEY_VALUE_HEADS) * HEAD_WIDTH
    return (
        received[:, :query_columns],
        received[:, query_columns:rotated_columns],
        received[:, rotated_columns:],
    )


def solution(mesh):
    fine = Mesh(mesh.devices.reshape(2, 4, 2, 4, 2), ("xh", "y", "xl", "z", "c"))
    row, col = ("xh", "y"), ("xl", "z", "c")
    in_specs = (P(row, col), P(row, col), P(row))
    out_specs = (P(row + col, None),) * 3
    return jax.shard_map(shards, mesh=fine, in_specs=in_specs, out_specs=out_specs, check_vma=False)
```

```python
import math

import jax
import jax.numpy as jnp
import numpy as np
from jax import lax
from jax.experimental import pallas as pl
from jax.experimental.pallas import tpu as pltpu
from jax.sharding import Mesh
from jax.sharding import PartitionSpec as P

HEAD_WIDTH = 128
QUERY_HEADS = 48
KEY_VALUE_HEADS = 8

rope_base = 1000000.0
SWAP = ((0, 1), (1, 0))


def rotary_tables(positions, head_size):
    half_size = head_size // 2
    column_ids = jnp.arange(head_size, dtype=jnp.int32)
    exponent = (column_ids % half_size).astype(jnp.float32) * (
        -2.0 * math.log(rope_base) / head_size
    )
    frequency = jnp.exp(exponent)
    angles = positions.astype(jnp.float32)[:, None] * frequency[None, :]
    sign_table = jnp.where(column_ids < half_size, -1.0, 1.0).astype(jnp.float32)
    return (jnp.cos(angles), jnp.sin(angles) * sign_table[None, :])


def ring_step(block, axis, way=1):
    pairs = [
        (i * 2 + c, ((i + (1, -1)[c] * way) % 4) * 2 + c) for i in range(4) for c in range(2)
    ]
    return lax.ppermute(block, (axis, "c"), pairs)


def piece_table():
    table = np.zeros((2, 4, 2, 4, 2, 8, 2), np.int32)
    for xh, y, xl, z, c in np.ndindex(2, 4, 2, 4, 2):
        way = (1, -1)[c]
        places = (0, -way, way, 2)
        a_blocks = {(xl ^ p, (z + d) % 4): p * 4 + i for p in range(2) for i, d in enumerate(places)}
        b_blocks = {(xh ^ p, (y + d) % 4): p * 4 + i for p in range(2) for i, d in enumerate(places)}
        pairs = [(a_blocks[f], b_blocks[f]) for f in np.ndindex(2, 4)]
        table[xh, y, xl, z, c] = sorted(pairs, key=lambda p: (7 in p, max(p), p))
    return table


TABLE = piece_table()
EARLY = 6


def product(table, first, count, a_blocks, b_blocks, parts, totals=()):
    depth = a_blocks[0][0].shape[1]
    rows = sum(v.shape[0] for v in a_blocks[0])
    width = b_blocks[0].shape[1] // 2
    slots = 2
    used_a = [p for p in range(len(a_blocks)) if a_blocks[p] is not None]
    used_b = [q for q in range(len(b_blocks)) if b_blocks[q] is not None]
    low, high = parts[0] * width, (parts[-1] + 1) * width

    def kernel(table_ref, *refs):
        refs = list(refs)
        a_refs = {p: [refs.pop(0) for _ in a_blocks[p]] for p in used_a}
        b_refs = {q: refs.pop(0) for q in used_b}
        total_refs = [refs.pop(0) for _ in totals]
        out_refs = [refs.pop(0) for _ in parts]
        a_buf, b_buf, sems = refs

        def start(k):
            slot = lax.rem(k, slots)
            a_id = table_ref[(first + k) * 2]
            b_id = table_ref[(first + k) * 2 + 1]
            for p in used_a:

                @pl.when(a_id == p)
                def _():
                    row = 0
                    for ref in a_refs[p]:
                        pltpu.make_async_copy(
                            ref, a_buf.at[slot, pl.ds(row, ref.shape[0]), :], sems.at[slot]
                        ).start()
                        row += ref.shape[0]

            for q in used_b:

                @pl.when(b_id == q)
                def _():
                    pltpu.make_async_copy(
                        b_refs[q].at[:, pl.ds(low, high - low)], b_buf.at[slot], sems.at[slot]
                    ).start()

        def wait(k):
            slot = lax.rem(k, slots)
            pltpu.make_async_copy(a_buf.at[slot], a_buf.at[slot], sems.at[slot]).wait()
            pltpu.make_async_copy(b_buf.at[slot], b_buf.at[slot], sems.at[slot]).wait()

        start(0)
        if totals:
            out_refs[0][...] = sum(ref[...] for ref in total_refs)
        else:
            for ref in out_refs:
                ref[...] = jnp.zeros(ref.shape, jnp.float32)

        @pl.loop(0, count)
        def _(k):
            @pl.when(k + 1 < count)
            def _():
                start(k + 1)

            wait(k)
            slot = lax.rem(k, slots)
            for i, ref in enumerate(out_refs):
                ref[...] += jnp.dot(
                    a_buf[slot],
                    b_buf[slot, :, i * width : (i + 1) * width],
                    preferred_element_type=jnp.float32,
                )

    anywhere = pl.BlockSpec(memory_space=pl.ANY)
    vmem = pl.BlockSpec(memory_space=pltpu.VMEM)
    pieces = [v for p in used_a for v in a_blocks[p]] + [b_blocks[q] for q in used_b]
    late = [7 in used_a and p == 7 for p in used_a for _ in a_blocks[p]] + [q == 7 for q in used_b]
    operands = [table.reshape(-1)]
    operands += [
        pltpu.with_memory_space_constraint(v, pltpu.VMEM if near else pltpu.HBM)
        for v, near in zip(pieces, late)
    ]
    return pl.pallas_call(
        kernel,
        out_shape=[jax.ShapeDtypeStruct((rows, width), jnp.float32) for _ in parts],
        in_specs=[pl.BlockSpec(memory_space=pltpu.SMEM)] + [anywhere] * len(pieces) + [vmem] * len(totals),
        out_specs=[vmem] * len(parts),
        scratch_shapes=[
            pltpu.VMEM((slots, rows, depth), pieces[0].dtype),
            pltpu.VMEM((slots, depth, high - low), pieces[0].dtype),
            pltpu.SemaphoreType.DMA((slots,)),
        ],
        compiler_params=pltpu.CompilerParams(vmem_limit_bytes=24 * 1024 * 1024),
        cost_estimate=pl.CostEstimate(
            flops=2 * rows * (high - low) * depth * count,
            bytes_accessed=(rows + high - low) * depth * 2 * count,
            transcendentals=0,
        ),
    )(*operands, *totals)


def turn(totals, cosine, sine):
    rows, columns = totals[0].shape
    tile = 256

    def kernel(*refs):
        *total_refs, cos_ref, sin_ref, out_ref = refs

        @pl.loop(0, rows // tile)
        def _(i):
            span = pl.ds(pl.multiple_of(i * tile, tile), tile)
            for h in range(columns // HEAD_WIDTH):
                lanes = slice(h * HEAD_WIDTH, (h + 1) * HEAD_WIDTH)
                head = sum(ref[span, lanes] for ref in total_refs)
                swapped = pltpu.roll(head, HEAD_WIDTH // 2, 1)
                out_ref[span, lanes] = (head * cos_ref[span, :] + swapped * sin_ref[span, :]).astype(
                    jnp.bfloat16
                )

    return pl.pallas_call(
        kernel,
        out_shape=jax.ShapeDtypeStruct((rows, columns), jnp.bfloat16),
        compiler_params=pltpu.CompilerParams(vmem_limit_bytes=24 * 1024 * 1024),
        cost_estimate=pl.CostEstimate(flops=rows * columns * 4, bytes_accessed=rows * columns * 12, transcendentals=0),
    )(*totals, cosine, sine)


def after(block, *before):
    return lax.optimization_barrier((block,) + before)[0]


def swap(block, axis):
    return lax.ppermute(block, axis, SWAP)


def gathers(a, b):
    part = a.shape[0] // 2

    z_near = ring_step(a, "z")
    p_0 = swap(a[:part], "xl")
    y_near = ring_step(b, "y")
    z_other = ring_step(a, "z", -1)
    y_other = ring_step(b, "y", -1)

    r = swap(after(b, p_0), "xh")
    p_0_near = ring_step(after(p_0, z_near), "z")
    p_0_other = ring_step(after(p_0, z_other), "z", -1)
    y_far = ring_step(after(y_near, y_other), "y")
    z_far = ring_step(after(z_near, p_0_near), "z")
    p_0_far = ring_step(after(p_0_near, p_0_other), "z")

    p_1 = swap(after(a[part:], r), "xl")
    r_near = ring_step(after(r, y_other), "y")
    r_other = ring_step(after(r, y_far), "y", -1)
    p_1_near = ring_step(after(p_1, z_far, p_0_far), "z")
    p_1_other = ring_step(after(p_1, z_far, p_0_far), "z", -1)
    r_far = ring_step(after(r_near, p_1_near), "y")
    p_1_far = ring_step(after(p_1_near, p_1_other), "z")

    a_blocks = [
        [a],
        [z_near],
        [z_other],
        [z_far],
        [p_0, p_1],
        [p_0_near, p_1_near],
        [p_0_other, p_1_other],
        [p_0_far, p_1_far],
    ]
    return a_blocks, [b, y_near, y_other, y_far, r, r_near, r_other, r_far]


def shards(tokens, joined_weight, positions):
    rows, depth = tokens.shape
    columns = joined_weight.shape[1]
    place = [lax.axis_index(a) for a in ("xh", "y", "xl", "z", "c")]
    table = jnp.asarray(TABLE)[tuple(place)]

    core = place[4]
    mine = lax.dynamic_slice_in_dim(joined_weight, core * depth, depth, 0)
    sent = lax.dynamic_slice_in_dim(joined_weight, (1 - core) * depth, depth, 0)
    weight = jnp.concatenate([mine, swap(sent, "c")], axis=1)
    a_blocks, b_blocks = gathers(tokens, weight)

    column_block = (place[2] * 4 + place[3]) * 2 + place[4]
    rotated = column_block * columns < (QUERY_HEADS + KEY_VALUE_HEADS) * HEAD_WIDTH
    cosine, sine = rotary_tables(positions, HEAD_WIDTH)
    cosine, sine = jnp.where(rotated, cosine, 1.0), jnp.where(rotated, sine, 0.0)

    early_a, early_b = a_blocks[:7] + [None], b_blocks[:7] + [None]
    table, cosine, sine = lax.optimization_barrier((table, cosine, sine))
    early, early_sent = product(table, 0, EARLY, early_a, early_b, (0, 1))
    early_received = swap(early_sent, "c")
    (late_sent,) = product(table, EARLY, 8 - EARLY, a_blocks, b_blocks, (1,))
    late_received = swap(late_sent, "c")
    (total,) = product(table, EARLY, 8 - EARLY, a_blocks, b_blocks, (0,), (early,))
    turned = turn([total, early_received, late_received], cosine, sine)
    received = lax.all_to_all(turned, ("xl", "z", "c"), split_axis=0, concat_axis=1, tiled=True)
    query_columns = QUERY_HEADS * HEAD_WIDTH
    rotated_columns = (QUERY_HEADS + KEY_VALUE_HEADS) * HEAD_WIDTH
    return (
        received[:, :query_columns],
        received[:, query_columns:rotated_columns],
        received[:, rotated_columns:],
    )


def solution(mesh):
    fine = Mesh(mesh.devices.reshape(2, 4, 2, 4, 2), ("xh", "y", "xl", "z", "c"))
    row, col = ("xh", "y"), ("xl", "z", "c")
    in_specs = (P(row, col), P(row, col), P(row))
    out_specs = (P(row + col, None),) * 3
    return jax.shard_map(shards, mesh=fine, in_specs=in_specs, out_specs=out_specs, check_vma=False)
```

```python
import math

import jax
import jax.numpy as jnp
import numpy as np
from jax import lax
from jax.experimental import pallas as pl
from jax.experimental.pallas import tpu as pltpu
from jax.sharding import Mesh
from jax.sharding import PartitionSpec as P

HEAD_WIDTH = 128
QUERY_HEADS = 48
KEY_VALUE_HEADS = 8

rope_base = 1000000.0
SWAP = ((0, 1), (1, 0))


def rotary_tables(positions, head_size):
    half_size = head_size // 2
    column_ids = jnp.arange(head_size, dtype=jnp.int32)
    exponent = (column_ids % half_size).astype(jnp.float32) * (
        -2.0 * math.log(rope_base) / head_size
    )
    frequency = jnp.exp(exponent)
    angles = positions.astype(jnp.float32)[:, None] * frequency[None, :]
    sign_table = jnp.where(column_ids < half_size, -1.0, 1.0).astype(jnp.float32)
    return (jnp.cos(angles), jnp.sin(angles) * sign_table[None, :])


def ring_step(block, axis, way=1):
    pairs = [
        (i * 2 + c, ((i + (1, -1)[c] * way) % 4) * 2 + c) for i in range(4) for c in range(2)
    ]
    return lax.ppermute(block, (axis, "c"), pairs)


def piece_table():
    table = np.zeros((2, 4, 2, 4, 2, 8, 2), np.int32)
    for xh, y, xl, z, c in np.ndindex(2, 4, 2, 4, 2):
        way = (1, -1)[c]
        places = (0, -way, way, 2)
        a_blocks = {(xl ^ p, (z + d) % 4): p * 4 + i for p in range(2) for i, d in enumerate(places)}
        b_blocks = {(xh ^ p, (y + d) % 4): p * 4 + i for p in range(2) for i, d in enumerate(places)}
        pairs = [(a_blocks[f], b_blocks[f]) for f in np.ndindex(2, 4)]
        table[xh, y, xl, z, c] = sorted(pairs, key=lambda p: (7 in p, max(p[0] > 4, p[1] > 4), max(p), p))
    return table


TABLE = piece_table()
FIRST, EARLY = 2, 6


def product(table, first, count, a_blocks, b_blocks, parts, totals=()):
    depth = a_blocks[0][0].shape[1]
    rows = sum(v.shape[0] for v in a_blocks[0])
    width = b_blocks[0][0].shape[1] // 2
    slots = 2
    used_a = [p for p in range(len(a_blocks)) if a_blocks[p] is not None]
    used_b = [q for q in range(len(b_blocks)) if b_blocks[q] is not None]
    low, high = parts[0] * width, (parts[-1] + 1) * width

    def kernel(table_ref, *refs):
        refs = list(refs)
        a_refs = {p: [refs.pop(0) for _ in a_blocks[p]] for p in used_a}
        b_refs = {q: [refs.pop(0) for _ in b_blocks[q]] for q in used_b}
        total_refs = [refs.pop(0) for _ in totals]
        out_refs = [refs.pop(0) for _ in parts]
        a_buf, b_buf, sems = refs

        def start(k):
            slot = lax.rem(k, slots)
            a_id = table_ref[(first + k) * 2]
            b_id = table_ref[(first + k) * 2 + 1]
            for p in used_a:

                @pl.when(a_id == p)
                def _():
                    row = 0
                    for ref in a_refs[p]:
                        pltpu.make_async_copy(
                            ref, a_buf.at[slot, pl.ds(row, ref.shape[0]), :], sems.at[slot]
                        ).start()
                        row += ref.shape[0]

            for q in used_b:

                @pl.when(b_id == q)
                def _():
                    row = 0
                    for ref in b_refs[q]:
                        pltpu.make_async_copy(
                            ref.at[:, pl.ds(low, high - low)],
                            b_buf.at[slot, pl.ds(row, ref.shape[0]), :],
                            sems.at[slot],
                        ).start()
                        row += ref.shape[0]

        def wait(k):
            slot = lax.rem(k, slots)
            pltpu.make_async_copy(a_buf.at[slot], a_buf.at[slot], sems.at[slot]).wait()
            pltpu.make_async_copy(b_buf.at[slot], b_buf.at[slot], sems.at[slot]).wait()

        start(0)
        for i, ref in enumerate(out_refs):
            ref[...] = total_refs[i][...] if totals else jnp.zeros(ref.shape, jnp.float32)

        @pl.loop(0, count)
        def _(k):
            @pl.when(k + 1 < count)
            def _():
                start(k + 1)

            wait(k)
            slot = lax.rem(k, slots)
            for i, ref in enumerate(out_refs):
                ref[...] += jnp.dot(
                    a_buf[slot],
                    b_buf[slot, :, i * width : (i + 1) * width],
                    preferred_element_type=jnp.float32,
                )

    anywhere = pl.BlockSpec(memory_space=pl.ANY)
    vmem = pl.BlockSpec(memory_space=pltpu.VMEM)
    pieces = [v for p in used_a for v in a_blocks[p]] + [v for q in used_b for v in b_blocks[q]]
    late = [p == 7 for p in used_a for _ in a_blocks[p]] + [q == 7 for q in used_b for _ in b_blocks[q]]
    operands = [table.reshape(-1)]
    operands += [
        pltpu.with_memory_space_constraint(v, pltpu.VMEM if near else pltpu.HBM)
        for v, near in zip(pieces, late)
    ]
    return pl.pallas_call(
        kernel,
        out_shape=[jax.ShapeDtypeStruct((rows, width), jnp.float32) for _ in parts],
        in_specs=[pl.BlockSpec(memory_space=pltpu.SMEM)] + [anywhere] * len(pieces) + [vmem] * len(totals),
        out_specs=[vmem] * len(parts),
        scratch_shapes=[
            pltpu.VMEM((slots, rows, depth), pieces[0].dtype),
            pltpu.VMEM((slots, depth, high - low), pieces[0].dtype),
            pltpu.SemaphoreType.DMA((slots,)),
        ],
        compiler_params=pltpu.CompilerParams(vmem_limit_bytes=24 * 1024 * 1024),
        cost_estimate=pl.CostEstimate(
            flops=2 * rows * (high - low) * depth * count,
            bytes_accessed=(rows + high - low) * depth * 2 * count,
            transcendentals=0,
        ),
    )(*operands, *totals)


def turn(totals, cosine, sine):
    rows, columns = totals[0].shape
    tile = 256

    def kernel(*refs):
        *total_refs, cos_ref, sin_ref, out_ref = refs

        @pl.loop(0, rows // tile)
        def _(i):
            span = pl.ds(pl.multiple_of(i * tile, tile), tile)
            for h in range(columns // HEAD_WIDTH):
                lanes = slice(h * HEAD_WIDTH, (h + 1) * HEAD_WIDTH)
                head = sum(ref[span, lanes] for ref in total_refs)
                swapped = pltpu.roll(head, HEAD_WIDTH // 2, 1)
                out_ref[span, lanes] = (head * cos_ref[span, :] + swapped * sin_ref[span, :]).astype(
                    jnp.bfloat16
                )

    return pl.pallas_call(
        kernel,
        out_shape=jax.ShapeDtypeStruct((rows, columns), jnp.bfloat16),
        compiler_params=pltpu.CompilerParams(vmem_limit_bytes=24 * 1024 * 1024),
        cost_estimate=pl.CostEstimate(flops=rows * columns * 4, bytes_accessed=rows * columns * 12, transcendentals=0),
    )(*totals, cosine, sine)


def after(block, *before):
    return lax.optimization_barrier((block,) + before)[0]


def swap(block, axis):
    return lax.ppermute(block, axis, SWAP)


def gathers(a, b, first_product, *early):
    part = a.shape[0] // 8 * 6

    z_near = ring_step(a, "z")
    p_0 = swap(a[:part], "xl")
    y_near = ring_step(b, "y")
    z_other = ring_step(a, "z", -1)
    y_other = ring_step(b, "y", -1)

    r = swap(after(b, p_0), "xh")
    p_0_near = ring_step(after(p_0, z_near), "z")
    p_0_other = ring_step(after(p_0, z_other), "z", -1)
    y_far = ring_step(after(y_near, y_other), "y")
    z_far = ring_step(after(z_near, p_0_near, *early), "z")
    p_0_far = ring_step(after(p_0_near, p_0_other), "z")

    p_1 = swap(after(a[part:], r), "xl")
    r_near = ring_step(after(r, y_other), "y")
    r_other = ring_step(after(r, y_far, p_1), "y", -1)
    split = b.shape[0] // 2
    r_far_1 = swap(after(y_far[split:], p_1), "xh")
    p_1_near = ring_step(after(p_1, z_far, p_0_far), "z")
    first = first_product([[a], [z_near], [z_other], [z_far], [p_0, p_1]], [[b], [y_near], [y_other], [y_far], [r]])
    p_1_other = ring_step(after(p_1, z_far, p_0_far, *first), "z", -1)
    p_1_far = ring_step(p_1_near, "z")
    r_far_0 = ring_step(after(r_near[:split], r_far_1), "y")
    r_far = [r_far_0, r_far_1]

    a_blocks = [
        [a],
        [z_near],
        [z_other],
        [z_far],
        [p_0, p_1],
        [p_0_near, p_1_near],
        [p_0_other, p_1_other],
        [p_0_far, p_1_far],
    ]
    return a_blocks, [[b], [y_near], [y_other], [y_far], [r], [r_near], [r_other], r_far], first


def shards(tokens, joined_weight, positions):
    rows, depth = tokens.shape
    columns = joined_weight.shape[1]
    place = [lax.axis_index(a) for a in ("xh", "y", "xl", "z", "c")]
    table = jnp.asarray(TABLE)[tuple(place)]

    core = place[4]
    mine = lax.dynamic_slice_in_dim(joined_weight, core * depth, depth, 0)
    sent = lax.dynamic_slice_in_dim(joined_weight, (1 - core) * depth, depth, 0)
    weight = jnp.concatenate([mine, swap(sent, "c")], axis=1)
    column_block = (place[2] * 4 + place[3]) * 2 + place[4]
    rotated = column_block * columns < (QUERY_HEADS + KEY_VALUE_HEADS) * HEAD_WIDTH
    cosine, sine = rotary_tables(positions, HEAD_WIDTH)
    cosine, sine = jnp.where(rotated, cosine, 1.0), jnp.where(rotated, sine, 0.0)
    table, cosine, sine = lax.optimization_barrier((table, cosine, sine))

    def first_product(first_a, first_b):
        return product(table, 0, FIRST, first_a, first_b, (0, 1))

    a_blocks, b_blocks, first = gathers(tokens, weight, first_product, table, cosine, sine)

    early_a, early_b = a_blocks[:7] + [None], b_blocks[:7] + [None]
    early, early_sent = product(table, FIRST, EARLY - FIRST, early_a, early_b, (0, 1), first)
    (sent,) = product(table, EARLY, 8 - EARLY, a_blocks, b_blocks, (1,), (early_sent,))
    from_sibling = swap(sent, "c")
    (total,) = product(table, EARLY, 8 - EARLY, a_blocks, b_blocks, (0,), (early,))
    turned = turn([total, from_sibling], cosine, sine)
    received = lax.all_to_all(turned, ("xl", "z", "c"), split_axis=0, concat_axis=1, tiled=True)
    query_columns = QUERY_HEADS * HEAD_WIDTH
    rotated_columns = (QUERY_HEADS + KEY_VALUE_HEADS) * HEAD_WIDTH
    return (
        received[:, :query_columns],
        received[:, query_columns:rotated_columns],
        received[:, rotated_columns:],
    )


def solution(mesh):
    fine = Mesh(mesh.devices.reshape(2, 4, 2, 4, 2), ("xh", "y", "xl", "z", "c"))
    row, col = ("xh", "y"), ("xl", "z", "c")
    in_specs = (P(row, col), P(row, col), P(row))
    out_specs = (P(row + col, None),) * 3
    return jax.shard_map(shards, mesh=fine, in_specs=in_specs, out_specs=out_specs, check_vma=False)
```

```python
import math

import jax
import jax.numpy as jnp
import numpy as np
from jax import lax
from jax.experimental import pallas as pl
from jax.experimental.pallas import tpu as pltpu
from jax.sharding import Mesh
from jax.sharding import PartitionSpec as P

HEAD_WIDTH = 128
QUERY_HEADS = 48
KEY_VALUE_HEADS = 8

rope_base = 1000000.0
SWAP = ((0, 1), (1, 0))


def rotary_tables(positions, head_size):
    half_size = head_size // 2
    column_ids = jnp.arange(head_size, dtype=jnp.int32)
    exponent = (column_ids % half_size).astype(jnp.float32) * (
        -2.0 * math.log(rope_base) / head_size
    )
    frequency = jnp.exp(exponent)
    angles = positions.astype(jnp.float32)[:, None] * frequency[None, :]
    sign_table = jnp.where(column_ids < half_size, -1.0, 1.0).astype(jnp.float32)
    return (jnp.cos(angles), jnp.sin(angles) * sign_table[None, :])


def ring_step(block, axis, way=1):
    pairs = [
        (i * 2 + c, ((i + (1, -1)[c] * way) % 4) * 2 + c) for i in range(4) for c in range(2)
    ]
    return lax.ppermute(block, (axis, "c"), pairs)


def piece_table():
    table = np.zeros((2, 4, 2, 4, 2, 8, 2), np.int32)
    for xh, y, xl, z, c in np.ndindex(2, 4, 2, 4, 2):
        way = (1, -1)[c]
        places = (0, -way, way, 2)
        a_blocks = {(xl ^ p, (z + d) % 4): p * 4 + i for p in range(2) for i, d in enumerate(places)}
        b_blocks = {(xh ^ p, (y + d) % 4): p * 4 + i for p in range(2) for i, d in enumerate(places)}
        pairs = [(a_blocks[f], b_blocks[f]) for f in np.ndindex(2, 4)]
        table[xh, y, xl, z, c] = sorted(pairs, key=lambda p: (7 in p, max(p[0] > 4, p[1] > 4), max(p), p))
    return table


TABLE = piece_table()
FIRST, EARLY = 2, 6


def product(table, first, count, a_blocks, b_blocks, parts, totals=()):
    depth = a_blocks[0][0].shape[1]
    rows = sum(v.shape[0] for v in a_blocks[0])
    width = b_blocks[0][0].shape[1] // 2
    slots = 2
    used_a = [p for p in range(len(a_blocks)) if a_blocks[p] is not None]
    used_b = [q for q in range(len(b_blocks)) if b_blocks[q] is not None]
    low, high = parts[0] * width, (parts[-1] + 1) * width

    def kernel(table_ref, *refs):
        refs = list(refs)
        a_refs = {p: [refs.pop(0) for _ in a_blocks[p]] for p in used_a}
        b_refs = {q: [refs.pop(0) for _ in b_blocks[q]] for q in used_b}
        total_refs = [refs.pop(0) for _ in totals]
        out_refs = [refs.pop(0) for _ in parts]
        a_buf, b_buf, sems = refs

        def start(k):
            slot = lax.rem(k, slots)
            a_id = table_ref[(first + k) * 2]
            b_id = table_ref[(first + k) * 2 + 1]
            for p in used_a:

                @pl.when(a_id == p)
                def _():
                    row = 0
                    for ref in a_refs[p]:
                        pltpu.make_async_copy(
                            ref, a_buf.at[slot, pl.ds(row, ref.shape[0]), :], sems.at[slot]
                        ).start()
                        row += ref.shape[0]

            for q in used_b:

                @pl.when(b_id == q)
                def _():
                    row = 0
                    for ref in b_refs[q]:
                        pltpu.make_async_copy(
                            ref.at[:, pl.ds(low, high - low)],
                            b_buf.at[slot, pl.ds(row, ref.shape[0]), :],
                            sems.at[slot],
                        ).start()
                        row += ref.shape[0]

        def wait(k):
            slot = lax.rem(k, slots)
            pltpu.make_async_copy(a_buf.at[slot], a_buf.at[slot], sems.at[slot]).wait()
            pltpu.make_async_copy(b_buf.at[slot], b_buf.at[slot], sems.at[slot]).wait()

        start(0)
        for i, ref in enumerate(out_refs):
            ref[...] = total_refs[i][...] if totals else jnp.zeros(ref.shape, jnp.float32)

        @pl.loop(0, count)
        def _(k):
            @pl.when(k + 1 < count)
            def _():
                start(k + 1)

            wait(k)
            slot = lax.rem(k, slots)
            for i, ref in enumerate(out_refs):
                ref[...] += jnp.dot(
                    a_buf[slot],
                    b_buf[slot, :, i * width : (i + 1) * width],
                    preferred_element_type=jnp.float32,
                )

    anywhere = pl.BlockSpec(memory_space=pl.ANY)
    vmem = pl.BlockSpec(memory_space=pltpu.VMEM)
    pieces = [v for p in used_a for v in a_blocks[p]] + [v for q in used_b for v in b_blocks[q]]
    late = [p == 7 for p in used_a for _ in a_blocks[p]] + [q == 7 for q in used_b for _ in b_blocks[q]]
    operands = [table.reshape(-1)]
    operands += [
        v if v is b_blocks[0][0] else pltpu.with_memory_space_constraint(v, pltpu.VMEM if near else pltpu.HBM)
        for v, near in zip(pieces, late)
    ]
    return pl.pallas_call(
        kernel,
        out_shape=[jax.ShapeDtypeStruct((rows, width), jnp.float32) for _ in parts],
        in_specs=[pl.BlockSpec(memory_space=pltpu.SMEM)] + [anywhere] * len(pieces) + [vmem] * len(totals),
        out_specs=[vmem] * len(parts),
        scratch_shapes=[
            pltpu.VMEM((slots, rows, depth), pieces[0].dtype),
            pltpu.VMEM((slots, depth, high - low), pieces[0].dtype),
            pltpu.SemaphoreType.DMA((slots,)),
        ],
        compiler_params=pltpu.CompilerParams(vmem_limit_bytes=24 * 1024 * 1024),
        cost_estimate=pl.CostEstimate(
            flops=2 * rows * (high - low) * depth * count,
            bytes_accessed=(rows + high - low) * depth * 2 * count,
            transcendentals=0,
        ),
    )(*operands, *totals)


def turn(totals, cosine, sine):
    rows, columns = totals[0].shape
    tile = 256

    def kernel(*refs):
        *total_refs, cos_ref, sin_ref, out_ref = refs

        @pl.loop(0, rows // tile)
        def _(i):
            span = pl.ds(pl.multiple_of(i * tile, tile), tile)
            for h in range(columns // HEAD_WIDTH):
                lanes = slice(h * HEAD_WIDTH, (h + 1) * HEAD_WIDTH)
                head = sum(ref[span, lanes] for ref in total_refs)
                swapped = pltpu.roll(head, HEAD_WIDTH // 2, 1)
                out_ref[span, lanes] = (head * cos_ref[span, :] + swapped * sin_ref[span, :]).astype(
                    jnp.bfloat16
                )

    return pl.pallas_call(
        kernel,
        out_shape=jax.ShapeDtypeStruct((rows, columns), jnp.bfloat16),
        compiler_params=pltpu.CompilerParams(vmem_limit_bytes=24 * 1024 * 1024),
        cost_estimate=pl.CostEstimate(flops=rows * columns * 4, bytes_accessed=rows * columns * 12, transcendentals=0),
    )(*totals, cosine, sine)


def after(block, *before):
    return lax.optimization_barrier((block,) + before)[0]


def swap(block, axis):
    return lax.ppermute(block, axis, SWAP)


def gathers(a, b, first_product, *early):
    part = a.shape[0] // 16 * 9

    z_near = ring_step(a, "z")
    p_0 = swap(a[:part], "xl")
    y_near = ring_step(b, "y")
    z_other = ring_step(a, "z", -1)
    y_other = ring_step(b, "y", -1)

    r = swap(after(b, p_0), "xh")
    p_0_near = ring_step(after(p_0, z_near), "z")
    p_0_other = ring_step(after(p_0, z_other), "z", -1)
    y_far = ring_step(after(y_near, y_other), "y")
    z_far = ring_step(after(z_near, p_0_near, *early), "z")
    p_0_far = ring_step(after(p_0_near, p_0_other), "z")

    p_1 = swap(after(a[part:], r), "xl")
    r_near = ring_step(after(r, y_other), "y")
    r_other = ring_step(after(r, y_far, p_1, p_0_other), "y", -1)
    split = b.shape[0] // 2
    r_far_1 = swap(after(y_far[split:], p_1), "xh")
    p_1_near = ring_step(after(p_1, z_far, p_0_far), "z")
    first = first_product([[a], [z_near], [z_other], [z_far], [p_0, p_1]], [[b], [y_near], [y_other], [y_far], [r]])
    p_1_other = ring_step(after(p_1, z_far, p_0_far, *first), "z", -1)
    p_1_far = ring_step(p_1_near, "z")
    r_far_0 = ring_step(r_near[:split], "y")
    r_far = [r_far_0, r_far_1]

    a_blocks = [
        [a],
        [z_near],
        [z_other],
        [z_far],
        [p_0, p_1],
        [p_0_near, p_1_near],
        [p_0_other, p_1_other],
        [p_0_far, p_1_far],
    ]
    return a_blocks, [[b], [y_near], [y_other], [y_far], [r], [r_near], [r_other], r_far], first


def shards(tokens, joined_weight, positions):
    rows, depth = tokens.shape
    columns = joined_weight.shape[1]
    place = [lax.axis_index(a) for a in ("xh", "y", "xl", "z", "c")]
    table = jnp.asarray(TABLE)[tuple(place)]

    core = place[4]
    mine = lax.dynamic_slice_in_dim(joined_weight, core * depth, depth, 0)
    sent = lax.dynamic_slice_in_dim(joined_weight, (1 - core) * depth, depth, 0)
    weight = jnp.concatenate([mine, swap(sent, "c")], axis=1)
    column_block = (place[2] * 4 + place[3]) * 2 + place[4]
    rotated = column_block * columns < (QUERY_HEADS + KEY_VALUE_HEADS) * HEAD_WIDTH
    cosine, sine = rotary_tables(positions, HEAD_WIDTH)
    cosine, sine = jnp.where(rotated, cosine, 1.0), jnp.where(rotated, sine, 0.0)
    table, cosine, sine = lax.optimization_barrier((table, cosine, sine))

    def first_product(first_a, first_b):
        return product(table, 0, FIRST, first_a, first_b, (0, 1))

    a_blocks, b_blocks, first = gathers(tokens, weight, first_product, table, cosine, sine)

    early_a, early_b = a_blocks[:7] + [None], b_blocks[:7] + [None]
    early, early_sent = product(table, FIRST, EARLY - FIRST, early_a, early_b, (0, 1), first)
    (sent,) = product(table, EARLY, 8 - EARLY, a_blocks, b_blocks, (1,), (early_sent,))
    from_sibling = swap(sent, "c")
    (total,) = product(table, EARLY, 8 - EARLY, a_blocks, b_blocks, (0,), (early,))
    turned = turn([total, from_sibling], cosine, sine)
    received = lax.all_to_all(turned, ("xl", "z", "c"), split_axis=0, concat_axis=1, tiled=True)
    query_columns = QUERY_HEADS * HEAD_WIDTH
    rotated_columns = (QUERY_HEADS + KEY_VALUE_HEADS) * HEAD_WIDTH
    return (
        received[:, :query_columns],
        received[:, query_columns:rotated_columns],
        received[:, rotated_columns:],
    )


def solution(mesh):
    fine = Mesh(mesh.devices.reshape(2, 4, 2, 4, 2), ("xh", "y", "xl", "z", "c"))
    row, col = ("xh", "y"), ("xl", "z", "c")
    in_specs = (P(row, col), P(row, col), P(row))
    out_specs = (P(row + col, None),) * 3
    return jax.shard_map(shards, mesh=fine, in_specs=in_specs, out_specs=out_specs, check_vma=False)
```

```python
import math

import jax
import jax.numpy as jnp
import numpy as np
from jax import lax
from jax.experimental import pallas as pl
from jax.experimental.pallas import tpu as pltpu
from jax.sharding import Mesh
from jax.sharding import PartitionSpec as P

HEAD_WIDTH = 128
QUERY_HEADS = 48
KEY_VALUE_HEADS = 8

rope_base = 1000000.0
SWAP = ((0, 1), (1, 0))


def rotary_tables(positions, head_size):
    half_size = head_size // 2
    column_ids = jnp.arange(head_size, dtype=jnp.int32)
    exponent = (column_ids % half_size).astype(jnp.float32) * (
        -2.0 * math.log(rope_base) / head_size
    )
    frequency = jnp.exp(exponent)
    angles = positions.astype(jnp.float32)[:, None] * frequency[None, :]
    sign_table = jnp.where(column_ids < half_size, -1.0, 1.0).astype(jnp.float32)
    return (jnp.cos(angles), jnp.sin(angles) * sign_table[None, :])


def ring_step(block, axis, way=1):
    pairs = [
        (i * 2 + c, ((i + (1, -1)[c] * way) % 4) * 2 + c) for i in range(4) for c in range(2)
    ]
    return lax.ppermute(block, (axis, "c"), pairs)


def piece_table():
    table = np.zeros((2, 4, 2, 4, 2, 8, 2), np.int32)
    for xh, y, xl, z, c in np.ndindex(2, 4, 2, 4, 2):
        way = (1, -1)[c]
        places = (0, -way, way, 2)
        a_blocks = {(xl ^ p, (z + d) % 4): p * 4 + i for p in range(2) for i, d in enumerate(places)}
        b_blocks = {(xh ^ p, (y + d) % 4): p * 4 + i for p in range(2) for i, d in enumerate(places)}
        pairs = [(a_blocks[f], b_blocks[f]) for f in np.ndindex(2, 4)]
        table[xh, y, xl, z, c] = sorted(pairs, key=lambda p: (7 in p, max(p[0] > 4, p[1] > 4), max(p), p))
    return table


TABLE = piece_table()
FIRST, EARLY = 2, 6


def product(table, first, count, a_blocks, b_blocks, parts, totals=()):
    depth = a_blocks[0][0].shape[1]
    rows = sum(v.shape[0] for v in a_blocks[0])
    width = b_blocks[0][0].shape[1] // 2
    slots = 2
    used_a = [p for p in range(len(a_blocks)) if a_blocks[p] is not None]
    used_b = [q for q in range(len(b_blocks)) if b_blocks[q] is not None]
    low, high = parts[0] * width, (parts[-1] + 1) * width

    def kernel(table_ref, *refs):
        refs = list(refs)
        a_refs = {p: [refs.pop(0) for _ in a_blocks[p]] for p in used_a}
        b_refs = {q: [refs.pop(0) for _ in b_blocks[q]] for q in used_b}
        total_refs = [refs.pop(0) for _ in totals]
        out_refs = [refs.pop(0) for _ in parts]
        a_buf, b_buf, sems = refs

        def start(k):
            slot = lax.rem(k, slots)
            a_id = table_ref[(first + k) * 2]
            b_id = table_ref[(first + k) * 2 + 1]
            for p in used_a:

                @pl.when(a_id == p)
                def _():
                    row = 0
                    for ref in a_refs[p]:
                        pltpu.make_async_copy(
                            ref, a_buf.at[slot, pl.ds(row, ref.shape[0]), :], sems.at[slot]
                        ).start()
                        row += ref.shape[0]

            for q in used_b:

                @pl.when(b_id == q)
                def _():
                    row = 0
                    for ref in b_refs[q]:
                        pltpu.make_async_copy(
                            ref.at[:, pl.ds(low, high - low)],
                            b_buf.at[slot, pl.ds(row, ref.shape[0]), :],
                            sems.at[slot],
                        ).start()
                        row += ref.shape[0]

        def wait(k):
            slot = lax.rem(k, slots)
            pltpu.make_async_copy(a_buf.at[slot], a_buf.at[slot], sems.at[slot]).wait()
            pltpu.make_async_copy(b_buf.at[slot], b_buf.at[slot], sems.at[slot]).wait()

        start(0)
        for i, ref in enumerate(out_refs):
            ref[...] = total_refs[i][...] if totals else jnp.zeros(ref.shape, jnp.float32)

        @pl.loop(0, count)
        def _(k):
            @pl.when(k + 1 < count)
            def _():
                start(k + 1)

            wait(k)
            slot = lax.rem(k, slots)
            for i, ref in enumerate(out_refs):
                ref[...] += jnp.dot(
                    a_buf[slot],
                    b_buf[slot, :, i * width : (i + 1) * width],
                    preferred_element_type=jnp.float32,
                )

    anywhere = pl.BlockSpec(memory_space=pl.ANY)
    vmem = pl.BlockSpec(memory_space=pltpu.VMEM)
    pieces = [v for p in used_a for v in a_blocks[p]] + [v for q in used_b for v in b_blocks[q]]
    late = [p == 7 for p in used_a for _ in a_blocks[p]] + [q == 7 for q in used_b for _ in b_blocks[q]]
    operands = [table.reshape(-1)]
    operands += [
        v if v is b_blocks[0][0] else pltpu.with_memory_space_constraint(v, pltpu.VMEM if near else pltpu.HBM)
        for v, near in zip(pieces, late)
    ]
    return pl.pallas_call(
        kernel,
        out_shape=[jax.ShapeDtypeStruct((rows, width), jnp.float32) for _ in parts],
        in_specs=[pl.BlockSpec(memory_space=pltpu.SMEM)] + [anywhere] * len(pieces) + [vmem] * len(totals),
        out_specs=[vmem] * len(parts),
        scratch_shapes=[
            pltpu.VMEM((slots, rows, depth), pieces[0].dtype),
            pltpu.VMEM((slots, depth, high - low), pieces[0].dtype),
            pltpu.SemaphoreType.DMA((slots,)),
        ],
        compiler_params=pltpu.CompilerParams(vmem_limit_bytes=24 * 1024 * 1024),
        cost_estimate=pl.CostEstimate(
            flops=2 * rows * (high - low) * depth * count,
            bytes_accessed=(rows + high - low) * depth * 2 * count,
            transcendentals=0,
        ),
    )(*operands, *totals)


def turn(totals, cosine, sine):
    rows, columns = totals[0].shape
    tile = 256

    def kernel(*refs):
        *total_refs, cos_ref, sin_ref, out_ref = refs

        @pl.loop(0, rows // tile)
        def _(i):
            span = pl.ds(pl.multiple_of(i * tile, tile), tile)
            for h in range(columns // HEAD_WIDTH):
                lanes = slice(h * HEAD_WIDTH, (h + 1) * HEAD_WIDTH)
                head = sum(ref[span, lanes] for ref in total_refs)
                swapped = pltpu.roll(head, HEAD_WIDTH // 2, 1)
                out_ref[span, lanes] = (head * cos_ref[span, :] + swapped * sin_ref[span, :]).astype(
                    jnp.bfloat16
                )

    return pl.pallas_call(
        kernel,
        out_shape=jax.ShapeDtypeStruct((rows, columns), jnp.bfloat16),
        compiler_params=pltpu.CompilerParams(vmem_limit_bytes=24 * 1024 * 1024),
        cost_estimate=pl.CostEstimate(flops=rows * columns * 4, bytes_accessed=rows * columns * 12, transcendentals=0),
    )(*totals, cosine, sine)


def after(block, *before):
    return lax.optimization_barrier((block,) + before)[0]


def swap(block, axis):
    return lax.ppermute(block, axis, SWAP)


def gathers(a, b, first_product, *early):
    part = a.shape[0] // 16 * 9

    z_near = ring_step(a, "z")
    p_0 = swap(a[:part], "xl")
    y_near = ring_step(b, "y")
    z_other = ring_step(a, "z", -1)
    y_other = ring_step(b, "y", -1)

    r = swap(after(b, p_0), "xh")
    p_0_near = ring_step(after(p_0, z_near, *early), "z")
    p_0_other = ring_step(after(p_0, z_other), "z", -1)
    y_far = ring_step(after(y_near, y_other), "y")
    z_far = ring_step(after(z_near, p_0_near), "z")
    p_0_far = ring_step(after(p_0_near, p_0_other), "z")

    p_1 = swap(after(a[part:], r), "xl")
    r_near = ring_step(after(r, y_other), "y")
    r_other = ring_step(after(r, y_far, p_1, p_0_other), "y", -1)
    split = b.shape[0] // 2
    r_far_1 = swap(after(y_far[split:], p_1), "xh")
    p_1_near = ring_step(after(p_1, z_far, p_0_far), "z")
    first = first_product([[a], [z_near], [z_other], [z_far], [p_0, p_1]], [[b], [y_near], [y_other], [y_far], [r]])
    p_1_other = ring_step(after(p_1, z_far, p_0_far, *first), "z", -1)
    p_1_far = ring_step(p_1_near, "z")
    r_far_0 = ring_step(r_near[:split], "y")
    r_far = [r_far_0, r_far_1]

    a_blocks = [
        [a],
        [z_near],
        [z_other],
        [z_far],
        [p_0, p_1],
        [p_0_near, p_1_near],
        [p_0_other, p_1_other],
        [p_0_far, p_1_far],
    ]
    return a_blocks, [[b], [y_near], [y_other], [y_far], [r], [r_near], [r_other], r_far], first


def shards(tokens, joined_weight, positions):
    rows, depth = tokens.shape
    columns = joined_weight.shape[1]
    place = [lax.axis_index(a) for a in ("xh", "y", "xl", "z", "c")]
    table = jnp.asarray(TABLE)[tuple(place)]

    core = place[4]
    mine = lax.dynamic_slice_in_dim(joined_weight, core * depth, depth, 0)
    sent = lax.dynamic_slice_in_dim(joined_weight, (1 - core) * depth, depth, 0)
    weight = jnp.concatenate([mine, swap(sent, "c")], axis=1)
    column_block = (place[2] * 4 + place[3]) * 2 + place[4]
    rotated = column_block * columns < (QUERY_HEADS + KEY_VALUE_HEADS) * HEAD_WIDTH
    cosine, sine = rotary_tables(positions, HEAD_WIDTH)
    cosine, sine = jnp.where(rotated, cosine, 1.0), jnp.where(rotated, sine, 0.0)
    table, cosine, sine = lax.optimization_barrier((table, cosine, sine))

    def first_product(first_a, first_b):
        return product(table, 0, FIRST, first_a, first_b, (0, 1))

    a_blocks, b_blocks, first = gathers(tokens, weight, first_product, table, cosine, sine)

    early_a, early_b = a_blocks[:7] + [None], b_blocks[:7] + [None]
    early, early_sent = product(table, FIRST, EARLY - FIRST, early_a, early_b, (0, 1), first)
    (sent,) = product(table, EARLY, 8 - EARLY, a_blocks, b_blocks, (1,), (early_sent,))
    from_sibling = swap(sent, "c")
    (total,) = product(table, EARLY, 8 - EARLY, a_blocks, b_blocks, (0,), (early,))
    turned = turn([total, from_sibling], cosine, sine)
    received = lax.all_to_all(turned, ("xl", "z", "c"), split_axis=0, concat_axis=1, tiled=True)
    query_columns = QUERY_HEADS * HEAD_WIDTH
    rotated_columns = (QUERY_HEADS + KEY_VALUE_HEADS) * HEAD_WIDTH
    return (
        received[:, :query_columns],
        received[:, query_columns:rotated_columns],
        received[:, rotated_columns:],
    )


def solution(mesh):
    fine = Mesh(mesh.devices.reshape(2, 4, 2, 4, 2), ("xh", "y", "xl", "z", "c"))
    row, col = ("xh", "y"), ("xl", "z", "c")
    in_specs = (P(row, col), P(row, col), P(row))
    out_specs = (P(row + col, None),) * 3
    return jax.shard_map(shards, mesh=fine, in_specs=in_specs, out_specs=out_specs, check_vma=False)
```

```python
import math

import jax
import jax.numpy as jnp
import numpy as np
from jax import lax
from jax.experimental import pallas as pl
from jax.experimental.pallas import tpu as pltpu
from jax.sharding import Mesh
from jax.sharding import PartitionSpec as P

HEAD_WIDTH = 128
QUERY_HEADS = 48
KEY_VALUE_HEADS = 8

rope_base = 1000000.0
SWAP = ((0, 1), (1, 0))


def rotary_tables(positions, head_size):
    half_size = head_size // 2
    column_ids = jnp.arange(head_size, dtype=jnp.int32)
    exponent = (column_ids % half_size).astype(jnp.float32) * (
        -2.0 * math.log(rope_base) / head_size
    )
    frequency = jnp.exp(exponent)
    angles = positions.astype(jnp.float32)[:, None] * frequency[None, :]
    sign_table = jnp.where(column_ids < half_size, -1.0, 1.0).astype(jnp.float32)
    return (jnp.cos(angles), jnp.sin(angles) * sign_table[None, :])


def ring_step(block, axis, way=1):
    pairs = [
        (i * 2 + c, ((i + (1, -1)[c] * way) % 4) * 2 + c) for i in range(4) for c in range(2)
    ]
    return lax.ppermute(block, (axis, "c"), pairs)


def piece_table():
    table = np.zeros((2, 4, 2, 4, 2, 8, 2), np.int32)
    for xh, y, xl, z, c in np.ndindex(2, 4, 2, 4, 2):
        way = (1, -1)[c]
        places = (0, -way, way, 2)
        a_blocks = {(xl ^ p, (z + d) % 4): p * 4 + i for p in range(2) for i, d in enumerate(places)}
        b_blocks = {(xh ^ p, (y + d) % 4): p * 4 + i for p in range(2) for i, d in enumerate(places)}
        pairs = [(a_blocks[f], b_blocks[f]) for f in np.ndindex(2, 4)]
        table[xh, y, xl, z, c] = sorted(pairs, key=lambda p: (7 in p, max(p[0] > 4, p[1] > 4), max(p), p))
    return table


TABLE = piece_table()
FIRST, EARLY = 2, 6


def product(table, first, count, a_blocks, b_blocks, parts, totals=()):
    depth = a_blocks[0][0].shape[1]
    rows = sum(v.shape[0] for v in a_blocks[0])
    width = b_blocks[0][0].shape[1] // 2
    slots = 2
    used_a = [p for p in range(len(a_blocks)) if a_blocks[p] is not None]
    used_b = [q for q in range(len(b_blocks)) if b_blocks[q] is not None]
    low, high = parts[0] * width, (parts[-1] + 1) * width

    def kernel(table_ref, *refs):
        refs = list(refs)
        a_refs = {p: [refs.pop(0) for _ in a_blocks[p]] for p in used_a}
        b_refs = {q: [refs.pop(0) for _ in b_blocks[q]] for q in used_b}
        total_refs = [refs.pop(0) for _ in totals]
        out_refs = [refs.pop(0) for _ in parts]
        a_buf, b_buf, sems = refs

        def start(k):
            slot = lax.rem(k, slots)
            a_id = table_ref[(first + k) * 2]
            b_id = table_ref[(first + k) * 2 + 1]
            for p in used_a:

                @pl.when(a_id == p)
                def _():
                    row = 0
                    for ref in a_refs[p]:
                        pltpu.make_async_copy(
                            ref, a_buf.at[slot, pl.ds(row, ref.shape[0]), :], sems.at[slot]
                        ).start()
                        row += ref.shape[0]

            for q in used_b:

                @pl.when(b_id == q)
                def _():
                    row = 0
                    for ref in b_refs[q]:
                        pltpu.make_async_copy(
                            ref.at[:, pl.ds(low, high - low)],
                            b_buf.at[slot, pl.ds(row, ref.shape[0]), :],
                            sems.at[slot],
                        ).start()
                        row += ref.shape[0]

        def wait(k):
            slot = lax.rem(k, slots)
            pltpu.make_async_copy(a_buf.at[slot], a_buf.at[slot], sems.at[slot]).wait()
            pltpu.make_async_copy(b_buf.at[slot], b_buf.at[slot], sems.at[slot]).wait()

        start(0)
        for i, ref in enumerate(out_refs):
            ref[...] = total_refs[i][...] if totals else jnp.zeros(ref.shape, jnp.float32)

        @pl.loop(0, count)
        def _(k):
            @pl.when(k + 1 < count)
            def _():
                start(k + 1)

            wait(k)
            slot = lax.rem(k, slots)
            for i, ref in enumerate(out_refs):
                ref[...] += jnp.dot(
                    a_buf[slot],
                    b_buf[slot, :, i * width : (i + 1) * width],
                    preferred_element_type=jnp.float32,
                )

    anywhere = pl.BlockSpec(memory_space=pl.ANY)
    vmem = pl.BlockSpec(memory_space=pltpu.VMEM)
    pieces = [v for p in used_a for v in a_blocks[p]] + [v for q in used_b for v in b_blocks[q]]
    late = [p == 7 for p in used_a for _ in a_blocks[p]] + [q == 7 for q in used_b for _ in b_blocks[q]]
    operands = [table.reshape(-1)]
    operands += [
        v if v is b_blocks[0][0] else pltpu.with_memory_space_constraint(v, pltpu.VMEM if near else pltpu.HBM)
        for v, near in zip(pieces, late)
    ]
    return pl.pallas_call(
        kernel,
        out_shape=[jax.ShapeDtypeStruct((rows, width), jnp.float32) for _ in parts],
        in_specs=[pl.BlockSpec(memory_space=pltpu.SMEM)] + [anywhere] * len(pieces) + [vmem] * len(totals),
        out_specs=[vmem] * len(parts),
        scratch_shapes=[
            pltpu.VMEM((slots, rows, depth), pieces[0].dtype),
            pltpu.VMEM((slots, depth, high - low), pieces[0].dtype),
            pltpu.SemaphoreType.DMA((slots,)),
        ],
        compiler_params=pltpu.CompilerParams(vmem_limit_bytes=24 * 1024 * 1024),
        cost_estimate=pl.CostEstimate(
            flops=2 * rows * (high - low) * depth * count,
            bytes_accessed=(rows + high - low) * depth * 2 * count,
            transcendentals=0,
        ),
    )(*operands, *totals)


def turn(totals, cosine, sine):
    rows, columns = totals[0].shape
    tile = 256

    def kernel(*refs):
        *total_refs, cos_ref, sin_ref, out_ref = refs

        @pl.loop(0, rows // tile)
        def _(i):
            span = pl.ds(pl.multiple_of(i * tile, tile), tile)
            for h in range(columns // HEAD_WIDTH):
                lanes = slice(h * HEAD_WIDTH, (h + 1) * HEAD_WIDTH)
                head = sum(ref[span, lanes] for ref in total_refs)
                swapped = pltpu.roll(head, HEAD_WIDTH // 2, 1)
                out_ref[span, lanes] = (head * cos_ref[span, :] + swapped * sin_ref[span, :]).astype(
                    jnp.bfloat16
                )

    return pl.pallas_call(
        kernel,
        out_shape=jax.ShapeDtypeStruct((rows, columns), jnp.bfloat16),
        compiler_params=pltpu.CompilerParams(vmem_limit_bytes=24 * 1024 * 1024),
        cost_estimate=pl.CostEstimate(flops=rows * columns * 4, bytes_accessed=rows * columns * 12, transcendentals=0),
    )(*totals, cosine, sine)


def after(block, *before):
    return lax.optimization_barrier((block,) + before)[0]


def swap(block, axis):
    return lax.ppermute(block, axis, SWAP)


def gathers(a, b, first_product, *early):
    part = a.shape[0] // 16 * 9

    z_near = ring_step(a, "z")
    p_0 = swap(a[:part], "xl")
    y_near = ring_step(b, "y")
    z_other = ring_step(a, "z", -1)
    y_other = ring_step(b, "y", -1)

    r = swap(after(b, p_0), "xh")
    p_0_near = ring_step(after(p_0, z_near, *early), "z")
    p_0_other = ring_step(after(p_0, z_other), "z", -1)
    y_far = ring_step(after(y_near, y_other), "y")
    z_far = ring_step(after(z_near, p_0_near), "z")
    p_0_far = ring_step(after(p_0_near, p_0_other), "z")

    p_1 = swap(after(a[part:], r), "xl")
    r_near = ring_step(after(r, y_other), "y")
    r_other = ring_step(after(r, y_far, p_1), "y", -1)
    split = b.shape[0] // 2
    r_far_1 = swap(after(y_far[split:], p_1), "xh")
    p_1_near = ring_step(after(p_1, z_far, p_0_far), "z")
    first = first_product([[a], [z_near], [z_other], [z_far], [p_0, p_1]], [[b], [y_near], [y_other], [y_far], [r]])
    p_1_other = ring_step(after(p_1, z_far, p_0_far, *first), "z", -1)
    p_1_far = ring_step(p_1_near, "z")
    r_far_0 = ring_step(r_near[:split], "y")
    r_far = [r_far_0, r_far_1]

    a_blocks = [
        [a],
        [z_near],
        [z_other],
        [z_far],
        [p_0, p_1],
        [p_0_near, p_1_near],
        [p_0_other, p_1_other],
        [p_0_far, p_1_far],
    ]
    return a_blocks, [[b], [y_near], [y_other], [y_far], [r], [r_near], [r_other], r_far], first


def shards(tokens, joined_weight, positions):
    rows, depth = tokens.shape
    columns = joined_weight.shape[1]
    place = [lax.axis_index(a) for a in ("xh", "y", "xl", "z", "c")]
    table = jnp.asarray(TABLE)[tuple(place)]

    core = place[4]
    mine = lax.dynamic_slice_in_dim(joined_weight, core * depth, depth, 0)
    sent = lax.dynamic_slice_in_dim(joined_weight, (1 - core) * depth, depth, 0)
    weight = jnp.concatenate([mine, swap(sent, "c")], axis=1)
    column_block = (place[2] * 4 + place[3]) * 2 + place[4]
    rotated = column_block * columns < (QUERY_HEADS + KEY_VALUE_HEADS) * HEAD_WIDTH
    cosine, sine = rotary_tables(positions, HEAD_WIDTH)
    cosine, sine = jnp.where(rotated, cosine, 1.0), jnp.where(rotated, sine, 0.0)
    table, cosine, sine = lax.optimization_barrier((table, cosine, sine))

    def first_product(first_a, first_b):
        return product(table, 0, FIRST, first_a, first_b, (0, 1))

    a_blocks, b_blocks, first = gathers(tokens, weight, first_product, table, cosine, sine)

    early_a, early_b = a_blocks[:7] + [None], b_blocks[:7] + [None]
    early, early_sent = product(table, FIRST, EARLY - FIRST, early_a, early_b, (0, 1), first)
    (sent,) = product(table, EARLY, 8 - EARLY, a_blocks, b_blocks, (1,), (early_sent,))
    from_sibling = swap(sent, "c")
    (total,) = product(table, EARLY, 8 - EARLY, a_blocks, b_blocks, (0,), (early,))
    turned = turn([total, from_sibling], cosine, sine)
    received = lax.all_to_all(turned, ("xl", "z", "c"), split_axis=0, concat_axis=1, tiled=True)
    query_columns = QUERY_HEADS * HEAD_WIDTH
    rotated_columns = (QUERY_HEADS + KEY_VALUE_HEADS) * HEAD_WIDTH
    return (
        received[:, :query_columns],
        received[:, query_columns:rotated_columns],
        received[:, rotated_columns:],
    )


def solution(mesh):
    fine = Mesh(mesh.devices.reshape(2, 4, 2, 4, 2), ("xh", "y", "xl", "z", "c"))
    row, col = ("xh", "y"), ("xl", "z", "c")
    in_specs = (P(row, col), P(row, col), P(row))
    out_specs = (P(row + col, None),) * 3
    return jax.shard_map(shards, mesh=fine, in_specs=in_specs, out_specs=out_specs, check_vma=False)
```
